32 devices in a mesh: ta: 8 (over z, y), gz: 4 (over x, core).
Axes of the slice: x: 2, y: 2, z: 4, core: 2. Of those that a mesh axis runs over, the one named last changes fastest.
Arguments:
- eigvecs: bfloat16 [8, 2, 3, 16, 256, 128], P('ta', None, None, 'gz'), may hold values from -6 to 6
- gauge_links: bfloat16 [8, 3, 3, 3, 2, 16, 256], P('ta', None, None, None, None, 'gz'), may hold values from -2.5 to 2.5
- peramb: bfloat16 [8, 4, 4, 4, 2, 128, 128], P('ta', None, 'gz'), may hold values from -0.3984375 to 0.3984375
- momenta: int32 [2, 3], replicated, may hold values from -2 to 2
- disp_paths: int32 [2, 2], replicated, may hold values from 1 to 3, as said below
- sources: int32 [4], replicated, may hold values from 0 to 7
Outputs:
- elementals: bfloat16 [8, 2, 2, 2, 128, 128], P('ta', None, None, None, 'gz')
- correlator: float32 [4, 8, 2, 2, 2], P(None, 'ta')
The draws below stay inside these ranges and needn't reach their ends.
Inputs may be any that keep to these rules, and one draw needn't show every extreme that they name: `disp_paths`: in each momentum's row exactly one path runs along the third dimension (value 3); every other path is 1 or 2.
All inputs are finite; a program needn't handle non-finite values.
Results may differ from the reference program's by a relative error of at most 0.0081.
Values may be sent and summed in bfloat16 or wider, within the bound.
A program may use at most 128 MiB of HBM per device.

```python
import math
import jax
import jax.numpy as jnp
from jax import lax

NVEC = 128
LX = 16
LY = 16
NMOM = 2
NDISP = 2
NSRC = 4
NT = 8
LZ = 16
LXY = 256


def draw_disp_paths(key, part):
    chosen = jax.random.randint(jax.random.fold_in(key, 11), (NMOM, 1), 0, NDISP)
    others = jax.random.randint(jax.random.fold_in(key, 12), (NMOM, NDISP), 1, 3)
    slots = jnp.arange(NDISP, dtype=jnp.int32)[None, :]
    return jnp.where(slots == chosen, 3, others).astype(jnp.int32)


def plant(result, rng, low, top_value):
    longest = result.shape.index(max(result.shape))
    spots = []
    for shift in (0, 1):
        where = [jax.random.randint(jax.random.fold_in(rng, axis), (), 0, length) for axis, length in enumerate(result.shape)]
        where[longest] = (where[longest] + shift) % result.shape[longest]
        spots.append(tuple(where))
    return result.at[spots[0]].set(low).at[spots[1]].set(top_value)


def levels(key, shape, split, low, top_value):
    level = 1.0
    for dim, parts in split:
        steps = jax.random.uniform(jax.random.fold_in(jax.random.fold_in(key, 6), dim), (parts,), jnp.float32, low / len(split), top_value / len(split))
        level = level * jnp.repeat(jnp.exp(steps), shape[dim] // parts).reshape((-1,) + (1,) * (len(shape) - 1 - dim))
    return level


def noise(rng, dims, scale, reach, split=(), held_as=jnp.bfloat16):
    loudness = levels(rng, dims, split, -0.22, 0.18) if split else 1.0
    array = jax.random.normal(rng, dims, jnp.float32) * scale * loudness
    return jnp.minimum(jnp.maximum(array, -reach), reach).astype(held_as)


def setup_inputs(seed: int = 0) -> dict:
    streams_of = jax.random.split(jax.random.key(seed), 7)
    return {
        "eigvecs": noise(streams_of[0], (NT, 2, 3, LZ, LXY, NVEC), 1.0, 6.0, ((0, 8), (3, 4))),
        "gauge_links": noise(streams_of[1], (NT, 3, 3, 3, 2, LZ, LXY), 0.408, 2.5, ((0, 8), (5, 4))),
        "peramb": noise(streams_of[2], (NT, NSRC, 4, 4, 2, NVEC, NVEC), 0.0625, 0.3984375, ((0, 8), (2, 4))),
        "momenta": plant(jax.random.randint(streams_of[3], (NMOM, 3), -2, 3), jax.random.fold_in(streams_of[3], 1), -2, 2).astype(jnp.int32),
        "disp_paths": draw_disp_paths(jax.random.fold_in(streams_of[6], 71), 0),
        "sources": plant(jax.random.randint(streams_of[5], (NSRC,), 0, NT), jax.random.fold_in(streams_of[5], 1), 0, NT - 1).astype(jnp.int32),
    }


HIGHEST = lax.Precision.HIGHEST

def transport(link_dir, source):
    link_re = link_dir[:, :, 0].astype(jnp.float32)
    link_im = link_dir[:, :, 1].astype(jnp.float32)
    source_re = source[0].astype(jnp.float32)
    source_im = source[1].astype(jnp.float32)
    total_re = jnp.zeros(source_re.shape, jnp.float32)
    total_im = jnp.zeros(source_re.shape, jnp.float32)
    for colour in range(3):
        coef_re = link_re[:, colour][..., None]
        coef_im = link_im[:, colour][..., None]
        total_re = total_re + coef_re * source_re[colour][None] - coef_im * source_im[colour][None]
        total_im = total_im + coef_re * source_im[colour][None] + coef_im * source_re[colour][None]
    return jnp.stack([total_re, total_im])

def back_transport(link_dir, source):
    link_re = link_dir[:, :, 0].astype(jnp.float32)
    link_im = link_dir[:, :, 1].astype(jnp.float32)
    source_re = source[0].astype(jnp.float32)
    source_im = source[1].astype(jnp.float32)
    total_re = jnp.zeros(source_re.shape, jnp.float32)
    total_im = jnp.zeros(source_re.shape, jnp.float32)
    for colour in range(3):
        coef_re = link_re[colour][..., None]
        coef_im = link_im[colour][..., None]
        total_re = total_re + coef_re * source_re[colour][None] + coef_im * source_im[colour][None]
        total_im = total_im + coef_re * source_im[colour][None] - coef_im * source_re[colour][None]
    return jnp.stack([total_re, total_im])

def displaced_fields(vectors, links_slice):
    results = []
    for direction in range(3):
        axis_id = (3, 4, 2)[direction]
        link_dir = links_slice[direction]
        shifted_up = jnp.roll(vectors, -1, axis=axis_id)
        forward = transport(link_dir, shifted_up)
        backward = back_transport(link_dir, vectors).astype(jnp.bfloat16)
        behind = jnp.roll(backward, 1, axis=axis_id).astype(jnp.float32)
        results.append((forward - behind).astype(jnp.bfloat16))
    return jnp.stack(results)

def phase_table(momentum, zcoord, lz_total):
    xcoord = jnp.arange(LX, dtype=jnp.int32)
    ycoord = jnp.arange(LY, dtype=jnp.int32)
    volume = LX * LY * lz_total
    phase_int = momentum[0] * xcoord[None, :, None] * (LY * lz_total) + momentum[1] * ycoord[None, None, :] * (LX * lz_total) + momentum[2] * zcoord[:, None, None] * (LX * LY)
    phase_int = jnp.mod(phase_int, volume)
    angles = phase_int.astype(jnp.float32) * (2.0 * math.pi / volume)
    return (jnp.cos(angles), jnp.sin(angles))

def elementals_one(vectors, selected, momentum, zcoord, lz_total):
    cosine, sine_table = phase_table(momentum, zcoord, lz_total)
    cosine = cosine[None, :, :, :, None]
    sine_table = sine_table[None, :, :, :, None]
    vec_re = vectors[0].astype(jnp.float32)
    vec_im = vectors[1].astype(jnp.float32)
    phased = jnp.stack([vec_re * cosine - vec_im * sine_table, -(vec_re * sine_table + vec_im * cosine)]).astype(jnp.bfloat16)
    num_vec = vectors.shape[-1]
    phased_rows = phased.reshape(2, -1, num_vec)
    displaced_cols = selected.reshape(selected.shape[0], 2, -1, num_vec)
    products = jnp.einsum('asi,dbsj->aidbj', phased_rows.astype(jnp.float32), displaced_cols.astype(jnp.float32), precision=HIGHEST)
    real_part = products[0, :, :, 0] - products[1, :, :, 1]
    imag_part = products[0, :, :, 1] + products[1, :, :, 0]
    return jnp.transpose(jnp.stack([real_part, imag_part]), (2, 0, 1, 3))

def slice_elementals(vectors_flat, links_flat, momenta, disp_paths):
    vectors = vectors_flat.reshape(2, 3, LZ, LX, LY, NVEC)
    links_slice = links_flat.reshape(3, 3, 3, 2, LZ, LX, LY)
    displaced = displaced_fields(vectors, links_slice)
    zcoord = jnp.arange(LZ, dtype=jnp.int32)

    def one_momentum(pair):
        selected = jnp.take(displaced, pair[1] - 1, axis=0)
        return elementals_one(vectors, selected, pair[0], zcoord, LZ)
    partial_value = lax.map(one_momentum, (momenta, disp_paths))
    norm_scale = 1.0 / math.sqrt(12.0 * LX * LY * LZ)
    return (partial_value * norm_scale).astype(jnp.bfloat16)

def contraction(sink_phi, source_phi, peramb_slice):
    sink_side = jnp.einsum('mdail,kpqblj->mdaikpqbj', sink_phi.astype(jnp.float32), peramb_slice.astype(jnp.float32), precision=HIGHEST)
    sink_re = sink_side[:, :, 0, :, :, :, :, 0] - sink_side[:, :, 1, :, :, :, :, 1]
    sink_im = sink_side[:, :, 0, :, :, :, :, 1] + sink_side[:, :, 1, :, :, :, :, 0]
    source_side = jnp.einsum('kpqail,kmdblj->kpqaimdbj', peramb_slice.astype(jnp.float32), source_phi.astype(jnp.float32), precision=HIGHEST)
    image_re = source_side[:, :, :, 0, :, :, :, 0] - source_side[:, :, :, 1, :, :, :, 1]
    image_im = source_side[:, :, :, 0, :, :, :, 1] + source_side[:, :, :, 1, :, :, :, 0]
    real_sum = jnp.einsum('mdikabj,kabimdj->kmd', sink_re, image_re, precision=HIGHEST) + jnp.einsum('mdikabj,kabimdj->kmd', sink_im, image_im, precision=HIGHEST)
    imag_sum = jnp.einsum('mdikabj,kabimdj->kmd', sink_im, image_re, precision=HIGHEST) - jnp.einsum('mdikabj,kabimdj->kmd', sink_re, image_im, precision=HIGHEST)
    return jnp.stack([real_sum, imag_sum], axis=-1)

def reference(eigvecs, gauge_links, peramb, momenta, disp_paths, sources):
    elementals = lax.map(lambda slice_pair: slice_elementals(slice_pair[0], slice_pair[1], momenta, disp_paths), (eigvecs, gauge_links))
    source_phi = jnp.take(elementals, sources, axis=0)

    def one_sink(slice_pair):
        return contraction(slice_pair[0], source_phi, slice_pair[1])
    corr_terms = lax.map(one_sink, (elementals, peramb))
    correlator = jnp.transpose(corr_terms, (1, 0, 2, 3, 4)) / (8.0 * NVEC)
    return (elementals, correlator)
```

```python
import math

import jax
import jax.numpy as jnp
from jax import lax
from jax.experimental import pallas as pl
from jax.experimental.pallas import tpu as pltpu
from jax.sharding import PartitionSpec as P

LX = 16
LY = 16
F32 = jnp.float32
BF16 = jnp.bfloat16
VMEM_BYTES = 48 * 1024 * 1024


def shifted(block, axis, distance):
    n = lax.axis_size(axis)
    return lax.ppermute(block, axis, [(i, (i + distance) % n) for i in range(n)])


def swapped(block, axis, bit):
    n = lax.axis_size(axis)
    return lax.ppermute(block, axis, [(i, i ^ bit) for i in range(n)])


def phase_angles(momenta, zcoord, lz_total):
    xcoord = jnp.arange(LX, dtype=jnp.int32)
    ycoord = jnp.arange(LY, dtype=jnp.int32)
    volume = LX * LY * lz_total
    p = momenta[:, :, None, None, None]
    phase_int = (
        p[:, 0] * xcoord[None, None, :, None] * (LY * lz_total)
        + p[:, 1] * ycoord[None, None, None, :] * (LX * lz_total)
        + p[:, 2] * zcoord[None, :, None, None] * (LX * LY)
    )
    phase_int = jnp.mod(phase_int, volume)
    return phase_int.astype(F32) * (2.0 * math.pi / volume)


def elementals_kernel(paths, turn, vec, above, top, links, phases, out, shift_buf, moved, phased, spread, total):
    z = pl.program_id(0)
    last = pl.num_programs(0) - 1

    @pl.when(z < last)
    def _():
        shift_buf[...] = above[0, :, :, 0]

    @pl.when(z == last)
    def _():
        shift_buf[...] = top[...]

    coefs = links.shape[2]
    wide = coefs * 128
    chosen = lax.broadcasted_iota(jnp.int32, (coefs, wide), 1) // 128
    row = lax.broadcasted_iota(jnp.int32, (coefs, wide), 0)
    select = jnp.where(chosen == row, 1.0, 0.0).astype(BF16)

    for direction in range(3):
        spread[...] = lax.dot_general(
            links[direction, 0], select, (((0,), (0,)), ((), ())), preferred_element_type=F32
        )

        def one_line(x1, carry, direction=direction):
            here = pl.ds(pl.multiple_of(x1 * LY, LY), LY)
            if direction == 0:
                there = pl.ds(pl.multiple_of(lax.rem(x1 + 1, LX) * LY, LY), LY)
            else:
                there = here
            source = []
            for part in range(2):
                for colour in range(3):
                    if direction == 2:
                        tile = shift_buf[part, colour, here, :].astype(F32)
                    else:
                        tile = vec[0, part, colour, 0, there, :].astype(F32)
                    if direction == 1:
                        tile = pltpu.roll(tile, LY - 1, 0)
                    source.append(tile)
            for a in range(3):
                re = None
                im = None
                for b in range(3):
                    at = (a * 3 + b) * 2
                    c_re = spread[here, at * 128:(at + 1) * 128]
                    c_im = spread[here, (at + 1) * 128:(at + 2) * 128]
                    s_re, s_im = source[b], source[3 + b]
                    t_re = c_re * s_re - c_im * s_im
                    t_im = c_re * s_im + c_im * s_re
                    re = t_re if re is None else re + t_re
                    im = t_im if im is None else im + t_im
                rows = pl.ds(pl.multiple_of(a * LX * LY + x1 * LY, LY), LY)
                moved[direction, rows, 0:128] = re.astype(BF16)
                moved[direction, rows, 128:256] = im.astype(BF16)
            return carry

        lax.fori_loop(0, LX, one_line, 0, unroll=4)

    for m in range(2):
        def one_phase(x1, carry, m=m):
            here = pl.ds(pl.multiple_of(x1 * LY, LY), LY)
            cosine = jnp.broadcast_to(phases[0, here, 2 * m:2 * m + 1], (LY, 128))
            sine = jnp.broadcast_to(phases[0, here, 2 * m + 1:2 * m + 2], (LY, 128))
            for colour in range(3):
                v_re = vec[0, 0, colour, 0, here, :].astype(F32)
                v_im = vec[0, 1, colour, 0, here, :].astype(F32)
                rc, rs, ic, js = v_re * cosine, v_re * sine, v_im * cosine, v_im * sine
                rows = pl.ds(pl.multiple_of(colour * LX * LY + x1 * LY, LY), LY)
                phased[rows, 0:128] = (rc - js).astype(BF16)
                phased[rows, 128:256] = (-(rs + ic)).astype(BF16)
                phased[rows, 256:384] = (rc + js).astype(BF16)
                phased[rows, 384:512] = (rs - ic).astype(BF16)
            return carry

        lax.fori_loop(0, LX, one_phase, 0, unroll=4)
        for k in range(2):
            prod = lax.dot_general(
                phased[...], moved[paths[m, k] - 1], (((0,), (0,)), ((), ())), preferred_element_type=F32
            )

            @pl.when(z == 0)
            def _():
                total[m, k] = prod

            @pl.when(z > 0)
            def _():
                total[m, k] += prod

    @pl.when(z == last)
    def _():
        for m in range(2):
            for k in range(2):
                d = paths[m, k] - 1
                c, s = turn[m, 2 * d], turn[m, 2 * d + 1]
                f_re = total[m, k, 0:128, 0:128] - total[m, k, 128:256, 128:256]
                f_im = total[m, k, 0:128, 128:256] + total[m, k, 128:256, 0:128]
                g_re = (total[m, k, 256:384, 0:128] - total[m, k, 384:512, 128:256]).T
                g_im = (total[m, k, 256:384, 128:256] + total[m, k, 384:512, 0:128]).T
                out[m, k, 0] = f_re - (c * g_re - s * g_im)
                out[m, k, 1] = f_im + (c * g_im + s * g_re)


def partial_elementals(eigvecs, top, links, phases, turn, paths):
    z_depth = eigvecs.shape[3]
    sites, num_vec = eigvecs.shape[4:]
    smem = pl.BlockSpec(memory_space=pltpu.SMEM)
    plane = (1, 2, 3, 1, sites, num_vec)
    return pl.pallas_call(
        elementals_kernel,
        grid=(z_depth,),
        out_shape=jax.ShapeDtypeStruct((2, 2, 2, num_vec, num_vec), F32),
        in_specs=[
            smem,
            smem,
            pl.BlockSpec(plane, lambda z: (0, 0, 0, z, 0, 0)),
            pl.BlockSpec(plane, lambda z: (0, 0, 0, jnp.minimum(z + 1, z_depth - 1), 0, 0)),
            pl.BlockSpec((2, 3, sites, num_vec), lambda z: (0, 0, 0, 0)),
            pl.BlockSpec((3, 1) + links.shape[2:], lambda z: (0, z, 0, 0)),
            pl.BlockSpec((1,) + phases.shape[1:], lambda z: (z, 0, 0)),
        ],
        out_specs=pl.BlockSpec((2, 2, 2, num_vec, num_vec), lambda z: (0, 0, 0, 0, 0)),
        scratch_shapes=[
            pltpu.VMEM((2, 3, sites, num_vec), BF16),
            pltpu.VMEM((3, 3 * sites, 2 * num_vec), BF16),
            pltpu.VMEM((3 * sites, 4 * num_vec), BF16),
            pltpu.VMEM((sites, links.shape[2] * 128), F32),
            pltpu.VMEM((2, 2, 4 * num_vec, 2 * num_vec), F32),
        ],
        compiler_params=pltpu.CompilerParams(vmem_limit_bytes=VMEM_BYTES),
        cost_estimate=pl.CostEstimate(flops=4 * 10**9, bytes_accessed=4 * 10**6, transcendentals=0),
    )(paths, turn, eigvecs, eigvecs, top, links, phases)


def correlator_kernel(sink, source, peramb, out):
    n = sink.shape[-1]
    spins = peramb.shape[1]
    tau = [(peramb[0, b, 0], peramb[0, b, 1]) for b in range(spins)]
    right = jnp.concatenate(
        [jnp.concatenate([t[0] for t in tau], axis=1), jnp.concatenate([t[1] for t in tau], axis=1)], axis=0
    )
    left = jnp.concatenate([jnp.concatenate(t, axis=1) for t in tau], axis=0)
    for mk in range(sink.shape[0]):
        f_re, f_im = sink[mk, 0], sink[mk, 1]
        block = jnp.concatenate(
            [jnp.concatenate([f_re, -f_im], axis=1), jnp.concatenate([f_im, f_re], axis=1)], axis=0
        )
        sink_side = jnp.dot(block, right, preferred_element_type=F32)
        g_re, g_im = source[0, mk, 0], source[0, mk, 1]
        block = jnp.concatenate(
            [jnp.concatenate([g_re, g_im], axis=1), jnp.concatenate([-g_im, g_re], axis=1)], axis=0
        )
        image = jnp.dot(left, block, preferred_element_type=F32)
        real = jnp.zeros((8, n), F32)
        imag = jnp.zeros((8, n), F32)
        for b in range(spins):
            s_re = sink_side[0:n, b * n:(b + 1) * n]
            s_im = sink_side[n:2 * n, b * n:(b + 1) * n]
            i_re = image[b * n:(b + 1) * n, 0:n]
            i_im = image[b * n:(b + 1) * n, n:2 * n]
            real += jnp.sum((s_re * i_re + s_im * i_im).reshape(n // 8, 8, n), axis=0)
            imag += jnp.sum((s_im * i_re - s_re * i_im).reshape(n // 8, 8, n), axis=0)
        out[0, mk, 0] = real
        out[0, mk, 1] = imag


def correlator_terms(sink, source, peramb):
    slots, spins, _, n, _ = peramb.shape
    pairs = sink.shape[0]
    return pl.pallas_call(
        correlator_kernel,
        grid=(slots,),
        out_shape=jax.ShapeDtypeStruct((slots, pairs, 2, 8, n), F32),
        in_specs=[
            pl.BlockSpec((pairs, 2, n, n), lambda s: (0, 0, 0, 0)),
            pl.BlockSpec((1, pairs, 2, n, n), lambda s: (s, 0, 0, 0, 0)),
            pl.BlockSpec((1, spins, 2, n, n), lambda s: (s, 0, 0, 0, 0)),
        ],
        out_specs=pl.BlockSpec((1, pairs, 2, 8, n), lambda s: (s, 0, 0, 0, 0)),
        compiler_params=pltpu.CompilerParams(vmem_limit_bytes=VMEM_BYTES),
        cost_estimate=pl.CostEstimate(flops=3 * 10**9, bytes_accessed=4 * 10**6, transcendentals=0),
    )(sink, source, peramb)


def gather_rows(rows):
    me = lax.axis_index("gz")
    groups = lax.axis_size("gz")
    blocks = rows[..., None, :, :]
    bit = groups // 2
    while bit:
        other = swapped(blocks, "gz", bit)
        upper = (me // bit) % 2 == 1
        low = jnp.where(upper, other, blocks)
        high = jnp.where(upper, blocks, other)
        blocks = jnp.stack([low, high], axis=-3)
        shape = blocks.shape
        blocks = blocks.reshape(shape[:-4] + (shape[-4] * 2,) + shape[-2:])
        bit //= 2
    shape = blocks.shape
    return blocks.reshape(shape[:-3] + (shape[-3] * shape[-2], shape[-1]))


def on_device(eigvecs, gauge_links, peramb, momenta, disp_paths, sources):
    num_vec = eigvecs.shape[-1]
    z_depth = eigvecs.shape[3]
    sites = eigvecs.shape[4]
    groups = lax.axis_size("gz")
    me = lax.axis_index("gz")
    lz_total = z_depth * groups
    row_count = num_vec // groups

    top = shifted(eigvecs[0, :, :, 0], "gz", -1)
    links = gauge_links[0].reshape(3, 18, z_depth, sites).transpose(0, 2, 1, 3)
    zcoord = me * z_depth + jnp.arange(z_depth, dtype=jnp.int32)
    angles = phase_angles(momenta, zcoord, lz_total).reshape(2, z_depth, sites)
    phases = jnp.stack([jnp.cos(angles), jnp.sin(angles)], axis=1)
    phases = phases.reshape(4, z_depth, sites).transpose(1, 2, 0)
    step = momenta.astype(F32) * (2.0 * math.pi / jnp.array([LX, LY, lz_total], F32))
    turn = jnp.stack([jnp.cos(step), jnp.sin(step)], axis=-1).reshape(2, 6)
    partial_value = partial_elementals(eigvecs, top, links, phases, turn, disp_paths)

    def rows_of(index):
        return lax.dynamic_slice_in_dim(partial_value, index * row_count, row_count, 3)

    full_rows = rows_of(me)
    for distance in range(1, groups):
        full_rows = full_rows + shifted(rows_of((me + distance) % groups), "gz", distance)
    norm_scale = 1.0 / math.sqrt(12.0 * LX * LY * lz_total)
    rows_phi = (full_rows * norm_scale).astype(BF16)

    slices = lax.axis_size("ta")
    if slices <= 16:
        held = jnp.stack([rows_phi] + [shifted(rows_phi, "ta", d) for d in range(1, slices)])
        chosen = jnp.mod(lax.axis_index("ta") - sources, slices)
    else:
        held = lax.all_gather(rows_phi, "ta")
        chosen = sources
    source_phi = gather_rows(jnp.take(held, chosen, axis=0))
    sink_phi = gather_rows(rows_phi)

    sink_phi = sink_phi.reshape(4, 2, num_vec, num_vec)
    source_phi = source_phi.reshape(sources.shape[0], 4, 2, num_vec, num_vec)
    terms = correlator_terms(sink_phi, source_phi, peramb[0, :, 0])
    summed = lax.psum(jnp.sum(terms, axis=(-2, -1)), "gz") / (8.0 * num_vec)
    return (rows_phi[None], summed.reshape(-1, 1, 2, 2, 2))


def solution(mesh):
    placed = (
        P("ta", None, None, "gz", None, None),
        P("ta", None, None, None, None, "gz", None),
        P("ta", None, "gz", None, None, None, None),
        P(),
        P(),
        P(),
    )
    return jax.shard_map(
        on_device,
        mesh=mesh,
        in_specs=placed,
        out_specs=(P("ta", None, None, None, "gz", None), P(None, "ta", None, None, None)),
        check_vma=False,
    )
```

```python
import math

import jax
import jax.numpy as jnp
from jax import lax
from jax.experimental import pallas as pl
from jax.experimental.pallas import tpu as pltpu
from jax.sharding import PartitionSpec as P

LX = 16
LY = 16
F32 = jnp.float32
BF16 = jnp.bfloat16
UNROLL = 16
VMEM_BYTES = 48 * 1024 * 1024


def shifted(block, axis, distance):
    n = lax.axis_size(axis)
    return lax.ppermute(block, axis, [(i, (i + distance) % n) for i in range(n)])


def swapped(block, axis, bit):
    n = lax.axis_size(axis)
    return lax.ppermute(block, axis, [(i, i ^ bit) for i in range(n)])


def phase_angles(momenta, zcoord, lz_total):
    xcoord = jnp.arange(LX, dtype=jnp.int32)
    ycoord = jnp.arange(LY, dtype=jnp.int32)
    volume = LX * LY * lz_total
    p = momenta[:, :, None, None, None]
    phase_int = (
        p[:, 0] * xcoord[None, None, :, None] * (LY * lz_total)
        + p[:, 1] * ycoord[None, None, None, :] * (LX * lz_total)
        + p[:, 2] * zcoord[None, :, None, None] * (LX * LY)
    )
    phase_int = jnp.mod(phase_int, volume)
    return phase_int.astype(F32) * (2.0 * math.pi / volume)


def transport_plane(source_at, spread, moved, slot):
    def one_line(x1, carry):
        here = pl.ds(pl.multiple_of(x1 * LY, LY), LY)
        source = source_at(x1)
        for a in range(3):
            re = None
            im = None
            for b in range(3):
                at = (a * 3 + b) * 2
                c_re = spread[here, at * 128:(at + 1) * 128]
                c_im = spread[here, (at + 1) * 128:(at + 2) * 128]
                s_re, s_im = source[b], source[3 + b]
                t_re = c_re * s_re - c_im * s_im
                t_im = c_re * s_im + c_im * s_re
                re = t_re if re is None else re + t_re
                im = t_im if im is None else im + t_im
            rows = pl.ds(pl.multiple_of(a * LX * LY + x1 * LY, LY), LY)
            moved[slot, rows, 0:128] = re.astype(BF16)
            moved[slot, rows, 128:256] = im.astype(BF16)
        return carry

    lax.fori_loop(0, LX, one_line, 0, unroll=UNROLL)


def elementals_kernel(paths, turn, vec, above, top, links, phases, out, moved, phased, spread, total):
    z = pl.program_id(0)
    last = pl.num_programs(0) - 1
    at_top = z == last
    in_plane = [paths[m, 0] + paths[m, 1] - 4 for m in range(2)]

    coefs = links.shape[2]
    wide = coefs * 128
    chosen = lax.broadcasted_iota(jnp.int32, (coefs, wide), 1) // 128
    row = lax.broadcasted_iota(jnp.int32, (coefs, wide), 0)
    select = jnp.where(chosen == row, 1.0, 0.0).astype(BF16)

    def spread_links(slot, direction):
        spread[slot] = lax.dot_general(
            links[direction, 0], select, (((0,), (0,)), ((), ())), preferred_element_type=F32
        )

    def next_plane(x1):
        here = pl.ds(pl.multiple_of(x1 * LY, LY), LY)
        return [
            jnp.where(at_top, top[part, colour, here, :], above[0, part, colour, 0, here, :]).astype(F32)
            for part in range(2)
            for colour in range(3)
        ]

    def next_in_plane(direction):
        along_first = jnp.where(direction == 0, 1, 0)
        turned = jnp.where(direction == 0, 0, LY - 1)

        def source_at(x1):
            line = lax.rem(x1 + along_first, LX)
            there = pl.ds(pl.multiple_of(line * LY, LY), LY)
            return [
                pltpu.roll(vec[0, part, colour, 0, there, :].astype(F32), turned, 0)
                for part in range(2)
                for colour in range(3)
            ]

        return source_at

    def add_product(slot, lhs, rhs):
        prod = jnp.dot(lhs, rhs, preferred_element_type=F32)
        total[slot] = jnp.where(z == 0, prod, total[slot] + prod)

    sites = LX * LY
    for colour in range(3):
        v_re = vec[0, 0, colour, 0].astype(F32).T
        v_im = vec[0, 1, colour, 0].astype(F32).T
        columns = slice(colour * sites, (colour + 1) * sites)
        for m in range(2):
            cosine = phases[0, 2 * m:2 * m + 1, :]
            sine = phases[0, 2 * m + 1:2 * m + 2, :]
            rc, rs, ic, js = v_re * cosine, v_re * sine, v_im * cosine, v_im * sine
            phased[m, 0:128, columns] = (rc - js).astype(BF16)
            phased[m, 128:256, columns] = (-(rs + ic)).astype(BF16)
            phased[m, 256:384, columns] = (rc + js).astype(BF16)
            phased[m, 384:512, columns] = (rs - ic).astype(BF16)

    spread_links(2, 2)
    spread_links(0, in_plane[0])
    transport_plane(next_plane, spread.at[2], moved, 2)
    for m in range(2):
        add_product(2 + m, phased[m], moved[2])
    transport_plane(next_in_plane(in_plane[0]), spread.at[0], moved, 0)
    add_product(0, phased[0], moved[0])

    @pl.when(in_plane[1] != in_plane[0])
    def _():
        spread_links(1, in_plane[1])
        transport_plane(next_in_plane(in_plane[1]), spread.at[1], moved, 1)

    add_product(1, phased[1], moved[jnp.where(in_plane[1] != in_plane[0], 1, 0)])

    @pl.when(z == last)
    def _():
        for m in range(2):
            for k in range(2):
                d = paths[m, k] - 1
                slot = jnp.where(d == 2, 2 + m, m)
                c, s = turn[m, 2 * d], turn[m, 2 * d + 1]
                f_re = total[slot, 0:128, 0:128] - total[slot, 128:256, 128:256]
                f_im = total[slot, 0:128, 128:256] + total[slot, 128:256, 0:128]
                g_re = (total[slot, 256:384, 0:128] - total[slot, 384:512, 128:256]).T
                g_im = (total[slot, 256:384, 128:256] + total[slot, 384:512, 0:128]).T
                out[m, k, 0] = f_re - (c * g_re - s * g_im)
                out[m, k, 1] = f_im + (c * g_im + s * g_re)


def partial_elementals(eigvecs, top, links, phases, turn, paths):
    z_depth = eigvecs.shape[3]
    sites, num_vec = eigvecs.shape[4:]
    smem = pl.BlockSpec(memory_space=pltpu.SMEM)
    plane = (1, 2, 3, 1, sites, num_vec)
    return pl.pallas_call(
        elementals_kernel,
        grid=(z_depth,),
        out_shape=jax.ShapeDtypeStruct((2, 2, 2, num_vec, num_vec), F32),
        in_specs=[
            smem,
            smem,
            pl.BlockSpec(plane, lambda z: (0, 0, 0, z, 0, 0)),
            pl.BlockSpec(plane, lambda z: (0, 0, 0, jnp.minimum(z + 1, z_depth - 1), 0, 0)),
            pl.BlockSpec((2, 3, sites, num_vec), lambda z: (0, 0, 0, 0)),
            pl.BlockSpec((3, 1) + links.shape[2:], lambda z: (0, z, 0, 0)),
            pl.BlockSpec((1,) + phases.shape[1:], lambda z: (z, 0, 0)),
        ],
        out_specs=pl.BlockSpec((2, 2, 2, num_vec, num_vec), lambda z: (0, 0, 0, 0, 0)),
        scratch_shapes=[
            pltpu.VMEM((3, 3 * sites, 2 * num_vec), BF16),
            pltpu.VMEM((2, 4 * num_vec, 3 * sites), BF16),
            pltpu.VMEM((3, sites, links.shape[2] * 128), F32),
            pltpu.VMEM((4, 4 * num_vec, 2 * num_vec), F32),
        ],
        compiler_params=pltpu.CompilerParams(vmem_limit_bytes=VMEM_BYTES),
        cost_estimate=pl.CostEstimate(flops=4 * 10**9, bytes_accessed=4 * 10**6, transcendentals=0),
    )(paths, turn, eigvecs, eigvecs, top, links, phases)


def correlator_kernel(sink, source, peramb, out):
    n = sink.shape[-1]
    spins = peramb.shape[1]
    tau = [(peramb[0, b, 0], peramb[0, b, 1]) for b in range(spins)]
    right = jnp.concatenate(
        [jnp.concatenate([t[0] for t in tau], axis=1), jnp.concatenate([t[1] for t in tau], axis=1)], axis=0
    )
    left = jnp.concatenate([jnp.concatenate(t, axis=1) for t in tau], axis=0)
    for mk in range(sink.shape[0]):
        f_re, f_im = sink[mk, 0], sink[mk, 1]
        block = jnp.concatenate(
            [jnp.concatenate([f_re, -f_im], axis=1), jnp.concatenate([f_im, f_re], axis=1)], axis=0
        )
        sink_side = jnp.dot(block, right, preferred_element_type=F32)
        g_re, g_im = source[0, mk, 0], source[0, mk, 1]
        block = jnp.concatenate(
            [jnp.concatenate([g_re, g_im], axis=1), jnp.concatenate([-g_im, g_re], axis=1)], axis=0
        )
        image = jnp.dot(left, block, preferred_element_type=F32)
        real = jnp.zeros((8, n), F32)
        imag = jnp.zeros((8, n), F32)
        for b in range(spins):
            s_re = sink_side[0:n, b * n:(b + 1) * n]
            s_im = sink_side[n:2 * n, b * n:(b + 1) * n]
            i_re = image[b * n:(b + 1) * n, 0:n]
            i_im = image[b * n:(b + 1) * n, n:2 * n]
            real += jnp.sum((s_re * i_re + s_im * i_im).reshape(n // 8, 8, n), axis=0)
            imag += jnp.sum((s_im * i_re - s_re * i_im).reshape(n // 8, 8, n), axis=0)
        out[0, mk, 0] = real
        out[0, mk, 1] = imag


def correlator_terms(sink, source, peramb):
    slots, spins, _, n, _ = peramb.shape
    pairs = sink.shape[0]
    return pl.pallas_call(
        correlator_kernel,
        grid=(slots,),
        out_shape=jax.ShapeDtypeStruct((slots, pairs, 2, 8, n), F32),
        in_specs=[
            pl.BlockSpec((pairs, 2, n, n), lambda s: (0, 0, 0, 0)),
            pl.BlockSpec((1, pairs, 2, n, n), lambda s: (s, 0, 0, 0, 0)),
            pl.BlockSpec((1, spins, 2, n, n), lambda s: (s, 0, 0, 0, 0)),
        ],
        out_specs=pl.BlockSpec((1, pairs, 2, 8, n), lambda s: (s, 0, 0, 0, 0)),
        compiler_params=pltpu.CompilerParams(vmem_limit_bytes=VMEM_BYTES),
        cost_estimate=pl.CostEstimate(flops=3 * 10**9, bytes_accessed=4 * 10**6, transcendentals=0),
    )(sink, source, peramb)


def gather_rows(rows):
    me = lax.axis_index("gz")
    groups = lax.axis_size("gz")
    blocks = rows[..., None, :, :]
    bit = groups // 2
    while bit:
        other = swapped(blocks, "gz", bit)
        upper = (me // bit) % 2 == 1
        low = jnp.where(upper, other, blocks)
        high = jnp.where(upper, blocks, other)
        blocks = jnp.stack([low, high], axis=-3)
        shape = blocks.shape
        blocks = blocks.reshape(shape[:-4] + (shape[-4] * 2,) + shape[-2:])
        bit //= 2
    shape = blocks.shape
    return blocks.reshape(shape[:-3] + (shape[-3] * shape[-2], shape[-1]))


def on_device(eigvecs, gauge_links, peramb, momenta, disp_paths, sources):
    num_vec = eigvecs.shape[-1]
    z_depth = eigvecs.shape[3]
    sites = eigvecs.shape[4]
    groups = lax.axis_size("gz")
    me = lax.axis_index("gz")
    lz_total = z_depth * groups
    row_count = num_vec // groups

    top = shifted(eigvecs[0, :, :, 0], "gz", -1)
    links = gauge_links[0].reshape(3, 18, z_depth, sites).transpose(0, 2, 1, 3)
    zcoord = me * z_depth + jnp.arange(z_depth, dtype=jnp.int32)
    angles = phase_angles(momenta, zcoord, lz_total).reshape(2, z_depth, sites)
    phases = jnp.stack([jnp.cos(angles), jnp.sin(angles)], axis=1)
    phases = phases.reshape(4, z_depth, sites).transpose(1, 0, 2)
    step = momenta.astype(F32) * (2.0 * math.pi / jnp.array([LX, LY, lz_total], F32))
    turn = jnp.stack([jnp.cos(step), jnp.sin(step)], axis=-1).reshape(2, 6)
    partial_value = partial_elementals(eigvecs, top, links, phases, turn, disp_paths)

    def rows_of(index):
        return lax.dynamic_slice_in_dim(partial_value, index * row_count, row_count, 3)

    full_rows = rows_of(me)
    for distance in range(1, groups):
        full_rows = full_rows + shifted(rows_of((me + distance) % groups), "gz", distance)
    norm_scale = 1.0 / math.sqrt(12.0 * LX * LY * lz_total)
    rows_phi = (full_rows * norm_scale).astype(BF16)

    slices = lax.axis_size("ta")
    if slices <= 16:
        held = jnp.stack([rows_phi] + [shifted(rows_phi, "ta", d) for d in range(1, slices)])
        chosen = jnp.mod(lax.axis_index("ta") - sources, slices)
    else:
        held = lax.all_gather(rows_phi, "ta")
        chosen = sources
    source_phi = gather_rows(jnp.take(held, chosen, axis=0))
    sink_phi = gather_rows(rows_phi)

    sink_phi = sink_phi.reshape(4, 2, num_vec, num_vec)
    source_phi = source_phi.reshape(sources.shape[0], 4, 2, num_vec, num_vec)
    terms = correlator_terms(sink_phi, source_phi, peramb[0, :, 0])
    summed = lax.psum(jnp.sum(terms, axis=(-2, -1)), "gz") / (8.0 * num_vec)
    return (rows_phi[None], summed.reshape(-1, 1, 2, 2, 2))


def solution(mesh):
    placed = (
        P("ta", None, None, "gz", None, None),
        P("ta", None, None, None, None, "gz", None),
        P("ta", None, "gz", None, None, None, None),
        P(),
        P(),
        P(),
    )
    return jax.shard_map(
        on_device,
        mesh=mesh,
        in_specs=placed,
        out_specs=(P("ta", None, None, None, "gz", None), P(None, "ta", None, None, None)),
        check_vma=False,
    )
```

```python
import functools
import math

import jax
import jax.numpy as jnp
from jax import lax
from jax.experimental import pallas as pl
from jax.experimental.pallas import tpu as pltpu
from jax.sharding import PartitionSpec as P

LX = 16
LY = 16
F32 = jnp.float32
BF16 = jnp.bfloat16
UNROLL = 16
VMEM_BYTES = 48 * 1024 * 1024


def shifted(block, axis, distance):
    n = lax.axis_size(axis)
    return lax.ppermute(block, axis, [(i, (i + distance) % n) for i in range(n)])


def swapped(block, axis, bit):
    n = lax.axis_size(axis)
    return lax.ppermute(block, axis, [(i, i ^ bit) for i in range(n)])


def phase_angles(momenta, zcoord, lz_total):
    xcoord = jnp.arange(LX, dtype=jnp.int32)
    ycoord = jnp.arange(LY, dtype=jnp.int32)
    volume = LX * LY * lz_total
    p = momenta[:, :, None, None, None]
    phase_int = (
        p[:, 0] * xcoord[None, None, :, None] * (LY * lz_total)
        + p[:, 1] * ycoord[None, None, None, :] * (LX * lz_total)
        + p[:, 2] * zcoord[None, :, None, None] * (LX * LY)
    )
    phase_int = jnp.mod(phase_int, volume)
    return phase_int.astype(F32) * (2.0 * math.pi / volume)


def transport_plane(source_at, spread, moved, slot):
    def one_line(x1, carry):
        here = pl.ds(pl.multiple_of(x1 * LY, LY), LY)
        source = source_at(x1)
        for a in range(3):
            re = None
            im = None
            for b in range(3):
                at = (a * 3 + b) * 2
                c_re = spread[here, at * 128:(at + 1) * 128]
                c_im = spread[here, (at + 1) * 128:(at + 2) * 128]
                s_re, s_im = source[b], source[3 + b]
                t_re = c_re * s_re - c_im * s_im
                t_im = c_re * s_im + c_im * s_re
                re = t_re if re is None else re + t_re
                im = t_im if im is None else im + t_im
            rows = pl.ds(pl.multiple_of(a * LX * LY + x1 * LY, LY), LY)
            moved[slot, rows, 0:128] = re.astype(BF16)
            moved[slot, rows, 128:256] = im.astype(BF16)
        return carry

    lax.fori_loop(0, LX, one_line, 0, unroll=UNROLL)


def elementals_kernel(paths, turn, vec, above, top, links, phases, out, moved, phased, spread, total):
    z = pl.program_id(0)
    last = pl.num_programs(0) - 1
    at_top = z == last
    in_plane = [paths[m, 0] + paths[m, 1] - 4 for m in range(2)]

    coefs = links.shape[2]
    wide = coefs * 128
    chosen = lax.broadcasted_iota(jnp.int32, (coefs, wide), 1) // 128
    row = lax.broadcasted_iota(jnp.int32, (coefs, wide), 0)
    select = jnp.where(chosen == row, 1.0, 0.0).astype(BF16)

    def spread_links(slot, direction):
        spread[slot] = lax.dot_general(
            links[direction, 0], select, (((0,), (0,)), ((), ())), preferred_element_type=F32
        )

    def next_plane(x1):
        here = pl.ds(pl.multiple_of(x1 * LY, LY), LY)
        return [
            jnp.where(at_top, top[part, colour, here, :], above[0, part, colour, 0, here, :]).astype(F32)
            for part in range(2)
            for colour in range(3)
        ]

    def next_in_plane(direction):
        along_first = jnp.where(direction == 0, 1, 0)
        turned = jnp.where(direction == 0, 0, LY - 1)

        def source_at(x1):
            line = lax.rem(x1 + along_first, LX)
            there = pl.ds(pl.multiple_of(line * LY, LY), LY)
            return [
                pltpu.roll(vec[0, part, colour, 0, there, :].astype(F32), turned, 0)
                for part in range(2)
                for colour in range(3)
            ]

        return source_at

    def add_product(slot, lhs, rhs):
        prod = jnp.dot(lhs, rhs, preferred_element_type=F32)
        total[slot] = jnp.where(z == 0, prod, total[slot] + prod)

    sites = LX * LY
    for colour in range(3):
        v_re = vec[0, 0, colour, 0].astype(F32).T
        v_im = vec[0, 1, colour, 0].astype(F32).T
        columns = slice(colour * sites, (colour + 1) * sites)
        for m in range(2):
            cosine = phases[0, 2 * m:2 * m + 1, :]
            sine = phases[0, 2 * m + 1:2 * m + 2, :]
            rc, rs, ic, js = v_re * cosine, v_re * sine, v_im * cosine, v_im * sine
            phased[m, 0:128, columns] = (rc - js).astype(BF16)
            phased[m, 128:256, columns] = (-(rs + ic)).astype(BF16)
            phased[m, 256:384, columns] = (rc + js).astype(BF16)
            phased[m, 384:512, columns] = (rs - ic).astype(BF16)

    spread_links(2, 2)
    spread_links(0, in_plane[0])
    transport_plane(next_plane, spread.at[2], moved, 2)
    for m in range(2):
        add_product(2 + m, phased[m], moved[2])
    transport_plane(next_in_plane(in_plane[0]), spread.at[0], moved, 0)
    add_product(0, phased[0], moved[0])

    @pl.when(in_plane[1] != in_plane[0])
    def _():
        spread_links(1, in_plane[1])
        transport_plane(next_in_plane(in_plane[1]), spread.at[1], moved, 1)

    add_product(1, phased[1], moved[jnp.where(in_plane[1] != in_plane[0], 1, 0)])

    @pl.when(z == last)
    def _():
        for m in range(2):
            for k in range(2):
                d = paths[m, k] - 1
                slot = jnp.where(d == 2, 2 + m, m)
                c, s = turn[m, 2 * d], turn[m, 2 * d + 1]
                f_re = total[slot, 0:128, 0:128] - total[slot, 128:256, 128:256]
                f_im = total[slot, 0:128, 128:256] + total[slot, 128:256, 0:128]
                g_re = (total[slot, 256:384, 0:128] - total[slot, 384:512, 128:256]).T
                g_im = (total[slot, 256:384, 128:256] + total[slot, 384:512, 0:128]).T
                out[m, k, 0] = f_re - (c * g_re - s * g_im)
                out[m, k, 1] = f_im + (c * g_im + s * g_re)


def partial_elementals(eigvecs, top, links, phases, turn, paths):
    z_depth = eigvecs.shape[3]
    sites, num_vec = eigvecs.shape[4:]
    smem = pl.BlockSpec(memory_space=pltpu.SMEM)
    plane = (1, 2, 3, 1, sites, num_vec)
    return pl.pallas_call(
        elementals_kernel,
        grid=(z_depth,),
        out_shape=jax.ShapeDtypeStruct((2, 2, 2, num_vec, num_vec), F32),
        in_specs=[
            smem,
            smem,
            pl.BlockSpec(plane, lambda z: (0, 0, 0, z, 0, 0)),
            pl.BlockSpec(plane, lambda z: (0, 0, 0, jnp.minimum(z + 1, z_depth - 1), 0, 0)),
            pl.BlockSpec((2, 3, sites, num_vec), lambda z: (0, 0, 0, 0)),
            pl.BlockSpec((3, 1) + links.shape[2:], lambda z: (0, z, 0, 0)),
            pl.BlockSpec((1,) + phases.shape[1:], lambda z: (z, 0, 0)),
        ],
        out_specs=pl.BlockSpec((2, 2, 2, num_vec, num_vec), lambda z: (0, 0, 0, 0, 0)),
        scratch_shapes=[
            pltpu.VMEM((3, 3 * sites, 2 * num_vec), BF16),
            pltpu.VMEM((2, 4 * num_vec, 3 * sites), BF16),
            pltpu.VMEM((3, sites, links.shape[2] * 128), F32),
            pltpu.VMEM((4, 4 * num_vec, 2 * num_vec), F32),
        ],
        compiler_params=pltpu.CompilerParams(vmem_limit_bytes=VMEM_BYTES),
        cost_estimate=pl.CostEstimate(flops=4 * 10**9, bytes_accessed=4 * 10**6, transcendentals=0),
    )(paths, turn, eigvecs, eigvecs, top, links, phases)


def correlator_kernel(picked, sink, source, peramb, out):
    n = sink.shape[-1]
    spins = peramb.shape[1]
    tau = [(peramb[0, b, 0], peramb[0, b, 1]) for b in range(spins)]
    right = jnp.concatenate(
        [jnp.concatenate([t[0] for t in tau], axis=1), jnp.concatenate([t[1] for t in tau], axis=1)], axis=0
    )
    left = jnp.concatenate([jnp.concatenate(t, axis=1) for t in tau], axis=0)
    for mk in range(sink.shape[1]):
        f_re, f_im = sink[0, mk, 0], sink[0, mk, 1]
        block = jnp.concatenate(
            [jnp.concatenate([f_re, -f_im], axis=1), jnp.concatenate([f_im, f_re], axis=1)], axis=0
        )
        sink_side = jnp.dot(block, right, preferred_element_type=F32)
        g_re, g_im = source[0, mk, 0], source[0, mk, 1]
        block = jnp.concatenate(
            [jnp.concatenate([g_re, g_im], axis=1), jnp.concatenate([-g_im, g_re], axis=1)], axis=0
        )
        image = jnp.dot(left, block, preferred_element_type=F32)
        real = jnp.zeros((8, n), F32)
        imag = jnp.zeros((8, n), F32)
        for b in range(spins):
            s_re = sink_side[0:n, b * n:(b + 1) * n]
            s_im = sink_side[n:2 * n, b * n:(b + 1) * n]
            i_re = image[b * n:(b + 1) * n, 0:n]
            i_im = image[b * n:(b + 1) * n, n:2 * n]
            real += jnp.sum((s_re * i_re + s_im * i_im).reshape(n // 8, 8, n), axis=0)
            imag += jnp.sum((s_im * i_re - s_re * i_im).reshape(n // 8, 8, n), axis=0)
        out[0, mk, 0] = real
        out[0, mk, 1] = imag


def correlator_terms(held, picked, peramb):
    slots, spins, _, n, _ = peramb.shape
    pairs = held.shape[1]
    slice_block = (1, pairs, 2, n, n)
    return pl.pallas_call(
        correlator_kernel,
        grid_spec=pltpu.PrefetchScalarGridSpec(
            num_scalar_prefetch=1,
            grid=(slots,),
            in_specs=[
                pl.BlockSpec(slice_block, lambda s, picked: (picked[0], 0, 0, 0, 0)),
                pl.BlockSpec(slice_block, lambda s, picked: (picked[s + 1], 0, 0, 0, 0)),
                pl.BlockSpec((1, spins, 2, n, n), lambda s, picked: (s, 0, 0, 0, 0)),
            ],
            out_specs=pl.BlockSpec((1, pairs, 2, 8, n), lambda s, picked: (s, 0, 0, 0, 0)),
        ),
        out_shape=jax.ShapeDtypeStruct((slots, pairs, 2, 8, n), F32),
        compiler_params=pltpu.CompilerParams(vmem_limit_bytes=VMEM_BYTES),
        cost_estimate=pl.CostEstimate(flops=3 * 10**9, bytes_accessed=4 * 10**6, transcendentals=0),
    )(picked, held, held, peramb)


def exchange_kernel(scale, slices, partial, rows_out, held, landed, red_send, red_recv, ta_send, ta_recv, x_send, x_recv, core_send, core_recv):
    t = lax.axis_index("ta")
    g = lax.axis_index("gz")
    count = rows_out.shape[1]
    mesh_id = pl.DeviceIdType.MESH

    barrier = pltpu.get_barrier_semaphore()
    for d in range(1, slices):
        pl.semaphore_signal(barrier, inc=1, device_id={"ta": (t + d) % slices}, device_id_type=mesh_id)
    for d in range(1, 4):
        pl.semaphore_signal(barrier, inc=1, device_id={"gz": (g + d) % 4}, device_id_type=mesh_id)
    pl.semaphore_wait(barrier, slices + 2)

    def rows_at(group):
        return pl.ds(pl.multiple_of(group * count, count), count)

    def send(source, target, send_sem, recv_sem, where):
        copy = pltpu.make_async_remote_copy(
            src_ref=source,
            dst_ref=target,
            send_sem=send_sem,
            recv_sem=recv_sem,
            device_id=where,
            device_id_type=mesh_id,
        )
        copy.start()
        return copy

    reduced = [
        send(
            partial.at[:, rows_at((g + d) % 4), :],
            landed.at[d - 1],
            red_send.at[d - 1],
            red_recv.at[d - 1],
            {"gz": (g + d) % 4},
        )
        for d in range(1, 4)
    ]
    full = partial[:, rows_at(g), :]
    for d in range(1, 4):
        reduced[d - 1].wait_recv()
        full = full + landed[d - 1]
    rows = (full * scale).astype(BF16)
    rows_out[...] = rows
    held[t, :, rows_at(g), :] = rows

    across = (g + 2) % 4
    beside = g + 1 - 2 * (g % 2)
    mine = held.at[t, :, rows_at(g), :]
    over_ta = [
        send(mine, mine, ta_send.at[d - 1], ta_recv.at[d - 1], {"ta": (t + d) % slices})
        for d in range(1, slices)
    ]
    over_x = []
    over_core = []
    for d in range(slices):
        if d:
            over_ta[d - 1].wait_recv()
        block = held.at[(t + slices - d) % slices, :, rows_at(g), :]
        over_x.append(send(block, block, x_send.at[d], x_recv.at[d], {"gz": across}))
        over_core.append(send(block, block, core_send.at[0, d], core_recv.at[0, d], {"gz": beside}))
    for d in range(slices):
        over_x[d].wait_recv()
        block = held.at[(t + slices - d) % slices, :, rows_at(across), :]
        over_core.append(send(block, block, core_send.at[1, d], core_recv.at[1, d], {"gz": beside}))
    for copy in over_core:
        copy.wait_recv()
    for copy in reduced + over_ta + over_x + over_core:
        copy.wait_send()


def exchange(partial_value, slices, scale):
    parts, num_vec, _ = partial_value.shape
    count = num_vec // 4
    whole = pl.BlockSpec(memory_space=pltpu.VMEM)
    dma = pltpu.SemaphoreType.DMA
    return pl.pallas_call(
        functools.partial(exchange_kernel, scale, slices),
        out_shape=[
            jax.ShapeDtypeStruct((parts, count, num_vec), BF16),
            jax.ShapeDtypeStruct((slices, parts, num_vec, num_vec), BF16),
        ],
        in_specs=[whole],
        out_specs=[whole, whole],
        scratch_shapes=[
            pltpu.VMEM((3, parts, count, num_vec), F32),
            dma((3,)),
            dma((3,)),
            dma((slices - 1,)),
            dma((slices - 1,)),
            dma((slices,)),
            dma((slices,)),
            dma((2, slices)),
            dma((2, slices)),
        ],
        compiler_params=pltpu.CompilerParams(
            collective_id=0, has_side_effects=True, vmem_limit_bytes=VMEM_BYTES
        ),
    )(partial_value)


def gather_rows(rows):
    me = lax.axis_index("gz")
    groups = lax.axis_size("gz")
    blocks = rows[..., None, :, :]
    bit = groups // 2
    while bit:
        other = swapped(blocks, "gz", bit)
        upper = (me // bit) % 2 == 1
        low = jnp.where(upper, other, blocks)
        high = jnp.where(upper, blocks, other)
        blocks = jnp.stack([low, high], axis=-3)
        shape = blocks.shape
        blocks = blocks.reshape(shape[:-4] + (shape[-4] * 2,) + shape[-2:])
        bit //= 2
    shape = blocks.shape
    return blocks.reshape(shape[:-3] + (shape[-3] * shape[-2], shape[-1]))


def on_device(eigvecs, gauge_links, peramb, momenta, disp_paths, sources):
    num_vec = eigvecs.shape[-1]
    z_depth = eigvecs.shape[3]
    sites = eigvecs.shape[4]
    groups = lax.axis_size("gz")
    me = lax.axis_index("gz")
    lz_total = z_depth * groups
    row_count = num_vec // groups

    top = shifted(eigvecs[0, :, :, 0], "gz", -1)
    links = gauge_links[0].reshape(3, 18, z_depth, sites).transpose(0, 2, 1, 3)
    zcoord = me * z_depth + jnp.arange(z_depth, dtype=jnp.int32)
    angles = phase_angles(momenta, zcoord, lz_total).reshape(2, z_depth, sites)
    phases = jnp.stack([jnp.cos(angles), jnp.sin(angles)], axis=1)
    phases = phases.reshape(4, z_depth, sites).transpose(1, 0, 2)
    step = momenta.astype(F32) * (2.0 * math.pi / jnp.array([LX, LY, lz_total], F32))
    turn = jnp.stack([jnp.cos(step), jnp.sin(step)], axis=-1).reshape(2, 6)
    partial_value = partial_elementals(eigvecs, top, links, phases, turn, disp_paths)

    norm_scale = 1.0 / math.sqrt(12.0 * LX * LY * lz_total)
    slices = lax.axis_size("ta")
    if slices <= 16 and groups == 4:
        rows_phi, held = exchange(partial_value.reshape(8, num_vec, num_vec), slices, norm_scale)
        rows_phi = rows_phi.reshape(2, 2, 2, row_count, num_vec)
    else:
        full_rows = lax.psum_scatter(partial_value, "gz", scatter_dimension=3, tiled=True)
        rows_phi = (full_rows * norm_scale).astype(BF16)
        held = gather_rows(lax.all_gather(rows_phi, "ta"))
    held = held.reshape(slices, 4, 2, num_vec, num_vec)
    picked = jnp.concatenate([lax.axis_index("ta")[None].astype(jnp.int32), sources])
    terms = correlator_terms(held, picked, peramb[0, :, 0])
    summed = lax.psum(jnp.sum(terms, axis=(-2, -1)), "gz") / (8.0 * num_vec)
    return (rows_phi[None], summed.reshape(-1, 1, 2, 2, 2))


def solution(mesh):
    placed = (
        P("ta", None, None, "gz", None, None),
        P("ta", None, None, None, None, "gz", None),
        P("ta", None, "gz", None, None, None, None),
        P(),
        P(),
        P(),
    )
    return jax.shard_map(
        on_device,
        mesh=mesh,
        in_specs=placed,
        out_specs=(P("ta", None, None, None, "gz", None), P(None, "ta", None, None, None)),
        check_vma=False,
    )
```

```python
import functools
import math

import jax
import jax.numpy as jnp
from jax import lax
from jax.experimental import pallas as pl
from jax.experimental.pallas import tpu as pltpu
from jax.sharding import PartitionSpec as P

LX = 16
LY = 16
F32 = jnp.float32
BF16 = jnp.bfloat16
UNROLL = 16
VMEM_BYTES = 48 * 1024 * 1024


def shifted(block, axis, distance):
    n = lax.axis_size(axis)
    return lax.ppermute(block, axis, [(i, (i + distance) % n) for i in range(n)])


def swapped(block, axis, bit):
    n = lax.axis_size(axis)
    return lax.ppermute(block, axis, [(i, i ^ bit) for i in range(n)])


def phase_angles(momenta, zcoord, lz_total):
    xcoord = jnp.arange(LX, dtype=jnp.int32)
    ycoord = jnp.arange(LY, dtype=jnp.int32)
    volume = LX * LY * lz_total
    p = momenta[:, :, None, None, None]
    phase_int = (
        p[:, 0] * xcoord[None, None, :, None] * (LY * lz_total)
        + p[:, 1] * ycoord[None, None, None, :] * (LX * lz_total)
        + p[:, 2] * zcoord[None, :, None, None] * (LX * LY)
    )
    phase_int = jnp.mod(phase_int, volume)
    return phase_int.astype(F32) * (2.0 * math.pi / volume)


def transport_plane(source_at, spread, moved, slot):
    def one_line(x1, carry):
        here = pl.ds(pl.multiple_of(x1 * LY, LY), LY)
        source = source_at(x1)
        for a in range(3):
            re = None
            im = None
            for b in range(3):
                at = (a * 3 + b) * 2
                c_re = spread[here, at * 128:(at + 1) * 128]
                c_im = spread[here, (at + 1) * 128:(at + 2) * 128]
                s_re, s_im = source[b], source[3 + b]
                t_re = c_re * s_re - c_im * s_im
                t_im = c_re * s_im + c_im * s_re
                re = t_re if re is None else re + t_re
                im = t_im if im is None else im + t_im
            rows = pl.ds(pl.multiple_of(a * LX * LY + x1 * LY, LY), LY)
            moved[slot, rows, 0:128] = re.astype(BF16)
            moved[slot, rows, 128:256] = im.astype(BF16)
        return carry

    lax.fori_loop(0, LX, one_line, 0, unroll=UNROLL)


def elementals_kernel(paths, turn, vec, above, top, links, phases, out, moved, phased, spread, total):
    z = pl.program_id(0)
    last = pl.num_programs(0) - 1
    at_top = z == last
    in_plane = [paths[m, 0] + paths[m, 1] - 4 for m in range(2)]

    coefs = links.shape[2]
    wide = coefs * 128
    chosen = lax.broadcasted_iota(jnp.int32, (coefs, wide), 1) // 128
    row = lax.broadcasted_iota(jnp.int32, (coefs, wide), 0)
    select = jnp.where(chosen == row, 1.0, 0.0).astype(BF16)

    def spread_links(slot, direction):
        spread[slot] = lax.dot_general(
            links[direction, 0], select, (((0,), (0,)), ((), ())), preferred_element_type=F32
        )

    def next_plane(x1):
        here = pl.ds(pl.multiple_of(x1 * LY, LY), LY)
        return [
            jnp.where(at_top, top[part, colour, here, :], above[0, part, colour, 0, here, :]).astype(F32)
            for part in range(2)
            for colour in range(3)
        ]

    def next_in_plane(direction):
        along_first = jnp.where(direction == 0, 1, 0)
        turned = jnp.where(direction == 0, 0, LY - 1)

        def source_at(x1):
            line = lax.rem(x1 + along_first, LX)
            there = pl.ds(pl.multiple_of(line * LY, LY), LY)
            return [
                pltpu.roll(vec[0, part, colour, 0, there, :].astype(F32), turned, 0)
                for part in range(2)
                for colour in range(3)
            ]

        return source_at

    def add_product(slot, lhs, rhs):
        prod = jnp.dot(lhs, rhs, preferred_element_type=F32)
        total[slot] = jnp.where(z == 0, prod, total[slot] + prod)

    sites = LX * LY
    for colour in range(3):
        v_re = vec[0, 0, colour, 0].astype(F32).T
        v_im = vec[0, 1, colour, 0].astype(F32).T
        columns = slice(colour * sites, (colour + 1) * sites)
        for m in range(2):
            cosine = phases[0, 2 * m:2 * m + 1, :]
            sine = phases[0, 2 * m + 1:2 * m + 2, :]
            rc, rs, ic, js = v_re * cosine, v_re * sine, v_im * cosine, v_im * sine
            phased[m, 0:128, columns] = (rc - js).astype(BF16)
            phased[m, 128:256, columns] = (-(rs + ic)).astype(BF16)
            phased[m, 256:384, columns] = (rc + js).astype(BF16)
            phased[m, 384:512, columns] = (rs - ic).astype(BF16)

    spread_links(2, 2)
    spread_links(0, in_plane[0])
    transport_plane(next_plane, spread.at[2], moved, 2)
    for m in range(2):
        add_product(2 + m, phased[m], moved[2])
    transport_plane(next_in_plane(in_plane[0]), spread.at[0], moved, 0)
    add_product(0, phased[0], moved[0])

    @pl.when(in_plane[1] != in_plane[0])
    def _():
        spread_links(1, in_plane[1])
        transport_plane(next_in_plane(in_plane[1]), spread.at[1], moved, 1)

    add_product(1, phased[1], moved[jnp.where(in_plane[1] != in_plane[0], 1, 0)])

    @pl.when(z == last)
    def _():
        for m in range(2):
            for k in range(2):
                d = paths[m, k] - 1
                slot = jnp.where(d == 2, 2 + m, m)
                c, s = turn[m, 2 * d], turn[m, 2 * d + 1]
                f_re = total[slot, 0:128, 0:128] - total[slot, 128:256, 128:256]
                f_im = total[slot, 0:128, 128:256] + total[slot, 128:256, 0:128]
                g_re = (total[slot, 256:384, 0:128] - total[slot, 384:512, 128:256]).T
                g_im = (total[slot, 256:384, 128:256] + total[slot, 384:512, 0:128]).T
                out[m, k, 0] = f_re - (c * g_re - s * g_im)
                out[m, k, 1] = f_im + (c * g_im + s * g_re)


def partial_elementals(eigvecs, top, links, phases, turn, paths):
    z_depth = eigvecs.shape[3]
    sites, num_vec = eigvecs.shape[4:]
    smem = pl.BlockSpec(memory_space=pltpu.SMEM)
    plane = (1, 2, 3, 1, sites, num_vec)
    return pl.pallas_call(
        elementals_kernel,
        grid=(z_depth,),
        out_shape=jax.ShapeDtypeStruct((2, 2, 2, num_vec, num_vec), F32),
        in_specs=[
            smem,
            smem,
            pl.BlockSpec(plane, lambda z: (0, 0, 0, z, 0, 0)),
            pl.BlockSpec(plane, lambda z: (0, 0, 0, jnp.minimum(z + 1, z_depth - 1), 0, 0)),
            pl.BlockSpec((2, 3, sites, num_vec), lambda z: (0, 0, 0, 0)),
            pl.BlockSpec((3, 1) + links.shape[2:], lambda z: (0, z, 0, 0)),
            pl.BlockSpec((1,) + phases.shape[1:], lambda z: (z, 0, 0)),
        ],
        out_specs=pl.BlockSpec((2, 2, 2, num_vec, num_vec), lambda z: (0, 0, 0, 0, 0)),
        scratch_shapes=[
            pltpu.VMEM((3, 3 * sites, 2 * num_vec), BF16),
            pltpu.VMEM((2, 4 * num_vec, 3 * sites), BF16),
            pltpu.VMEM((3, sites, links.shape[2] * 128), F32),
            pltpu.VMEM((4, 4 * num_vec, 2 * num_vec), F32),
        ],
        compiler_params=pltpu.CompilerParams(vmem_limit_bytes=VMEM_BYTES),
        cost_estimate=pl.CostEstimate(flops=4 * 10**9, bytes_accessed=4 * 10**6, transcendentals=0),
    )(paths, turn, eigvecs, eigvecs, top, links, phases)


def correlator_kernel(picked, sink, source, peramb, out):
    n = sink.shape[-1]
    spins = peramb.shape[1]
    tau = [(peramb[0, b, 0], peramb[0, b, 1]) for b in range(spins)]
    right = jnp.concatenate(
        [jnp.concatenate([t[0] for t in tau], axis=1), jnp.concatenate([t[1] for t in tau], axis=1)], axis=0
    )
    left = jnp.concatenate([jnp.concatenate(t, axis=1) for t in tau], axis=0)
    for mk in range(sink.shape[1]):
        f_re, f_im = sink[0, mk, 0], sink[0, mk, 1]
        block = jnp.concatenate(
            [jnp.concatenate([f_re, -f_im], axis=1), jnp.concatenate([f_im, f_re], axis=1)], axis=0
        )
        sink_side = jnp.dot(block, right, preferred_element_type=F32)
        g_re, g_im = source[0, mk, 0], source[0, mk, 1]
        block = jnp.concatenate(
            [jnp.concatenate([g_re, g_im], axis=1), jnp.concatenate([-g_im, g_re], axis=1)], axis=0
        )
        image = jnp.dot(left, block, preferred_element_type=F32)
        real = jnp.zeros((8, n), F32)
        imag = jnp.zeros((8, n), F32)
        for b in range(spins):
            s_re = sink_side[0:n, b * n:(b + 1) * n]
            s_im = sink_side[n:2 * n, b * n:(b + 1) * n]
            i_re = image[b * n:(b + 1) * n, 0:n]
            i_im = image[b * n:(b + 1) * n, n:2 * n]
            real += jnp.sum((s_re * i_re + s_im * i_im).reshape(n // 8, 8, n), axis=0)
            imag += jnp.sum((s_im * i_re - s_re * i_im).reshape(n // 8, 8, n), axis=0)
        out[0, mk, 0] = real
        out[0, mk, 1] = imag


def correlator_terms(held, picked, peramb):
    slots, spins, _, n, _ = peramb.shape
    pairs = held.shape[1]
    slice_block = (1, pairs, 2, n, n)
    return pl.pallas_call(
        correlator_kernel,
        grid_spec=pltpu.PrefetchScalarGridSpec(
            num_scalar_prefetch=1,
            grid=(slots,),
            in_specs=[
                pl.BlockSpec(slice_block, lambda s, picked: (picked[0], 0, 0, 0, 0)),
                pl.BlockSpec(slice_block, lambda s, picked: (picked[s + 1], 0, 0, 0, 0)),
                pl.BlockSpec((1, spins, 2, n, n), lambda s, picked: (s, 0, 0, 0, 0)),
            ],
            out_specs=pl.BlockSpec((1, pairs, 2, 8, n), lambda s, picked: (s, 0, 0, 0, 0)),
        ),
        out_shape=jax.ShapeDtypeStruct((slots, pairs, 2, 8, n), F32),
        compiler_params=pltpu.CompilerParams(vmem_limit_bytes=VMEM_BYTES),
        cost_estimate=pl.CostEstimate(flops=3 * 10**9, bytes_accessed=4 * 10**6, transcendentals=0),
    )(picked, held, held, peramb)


def exchange_kernel(scale, slices, partial, rows_out, held, landed, red_send, red_recv, ta_send, ta_recv, x_send, x_recv, core_send, core_recv):
    t = lax.axis_index("ta")
    g = lax.axis_index("gz")
    count = rows_out.shape[1]
    mesh_id = pl.DeviceIdType.MESH

    barrier = pltpu.get_barrier_semaphore()
    half = slices // 2
    pair = t + 1 - 2 * (t % 2)
    for where in [(t + 2 * d) % slices for d in range(1, half)] + [pair]:
        pl.semaphore_signal(barrier, inc=1, device_id={"ta": where}, device_id_type=mesh_id)
    for d in range(1, 4):
        pl.semaphore_signal(barrier, inc=1, device_id={"gz": (g + d) % 4}, device_id_type=mesh_id)
    pl.semaphore_wait(barrier, half + 3)

    def rows_at(group):
        return pl.ds(pl.multiple_of(group * count, count), count)

    def send(source, target, send_sem, recv_sem, where):
        copy = pltpu.make_async_remote_copy(
            src_ref=source,
            dst_ref=target,
            send_sem=send_sem,
            recv_sem=recv_sem,
            device_id=where,
            device_id_type=mesh_id,
        )
        copy.start()
        return copy

    reduced = [
        send(
            partial.at[:, rows_at((g + d) % 4), :],
            landed.at[d - 1],
            red_send.at[d - 1],
            red_recv.at[d - 1],
            {"gz": (g + d) % 4},
        )
        for d in range(1, 4)
    ]
    full = partial[:, rows_at(g), :]
    for d in range(1, 4):
        reduced[d - 1].wait_recv()
        full = full + landed[d - 1]
    rows = (full * scale).astype(BF16)
    rows_out[...] = rows
    held[t, :, rows_at(g), :] = rows

    across = (g + 2) % 4
    beside = g + 1 - 2 * (g % 2)
    mine = held.at[t, :, rows_at(g), :]
    over_ta = [
        send(mine, mine, ta_send.at[d - 1], ta_recv.at[d - 1], {"ta": (t + 2 * d) % slices})
        for d in range(1, half)
    ]
    over_pair = []
    over_x = []
    over_core = []

    def pass_on(n, block):
        over_x.append(send(block, block, x_send.at[n], x_recv.at[n], {"gz": across}))
        over_core.append(send(block, block, core_send.at[0, n], core_recv.at[0, n], {"gz": beside}))

    def slice_of(n):
        first = t if n < half else pair
        return (first + slices - 2 * (n % half)) % slices

    for n in range(half):
        if n:
            over_ta[n - 1].wait_recv()
        block = held.at[slice_of(n), :, rows_at(g), :]
        at = half - 1 + n
        over_pair.append(send(block, block, ta_send.at[at], ta_recv.at[at], {"ta": pair}))
        pass_on(n, block)
    for n in range(half, slices):
        over_pair[n - half].wait_recv()
        pass_on(n, held.at[slice_of(n), :, rows_at(g), :])
    for n in range(slices):
        over_x[n].wait_recv()
        block = held.at[slice_of(n), :, rows_at(across), :]
        over_core.append(send(block, block, core_send.at[1, n], core_recv.at[1, n], {"gz": beside}))
    for copy in over_core:
        copy.wait_recv()
    for copy in reduced + over_ta + over_pair + over_x + over_core:
        copy.wait_send()


def exchange(partial_value, slices, scale):
    parts, num_vec, _ = partial_value.shape
    count = num_vec // 4
    whole = pl.BlockSpec(memory_space=pltpu.VMEM)
    dma = pltpu.SemaphoreType.DMA
    return pl.pallas_call(
        functools.partial(exchange_kernel, scale, slices),
        out_shape=[
            jax.ShapeDtypeStruct((parts, count, num_vec), BF16),
            jax.ShapeDtypeStruct((slices, parts, num_vec, num_vec), BF16),
        ],
        in_specs=[whole],
        out_specs=[whole, whole],
        scratch_shapes=[
            pltpu.VMEM((3, parts, count, num_vec), F32),
            dma((3,)),
            dma((3,)),
            dma((slices - 1,)),
            dma((slices - 1,)),
            dma((slices,)),
            dma((slices,)),
            dma((2, slices)),
            dma((2, slices)),
        ],
        compiler_params=pltpu.CompilerParams(
            collective_id=0, has_side_effects=True, vmem_limit_bytes=VMEM_BYTES
        ),
    )(partial_value)


def gather_rows(rows):
    me = lax.axis_index("gz")
    groups = lax.axis_size("gz")
    blocks = rows[..., None, :, :]
    bit = groups // 2
    while bit:
        other = swapped(blocks, "gz", bit)
        upper = (me // bit) % 2 == 1
        low = jnp.where(upper, other, blocks)
        high = jnp.where(upper, blocks, other)
        blocks = jnp.stack([low, high], axis=-3)
        shape = blocks.shape
        blocks = blocks.reshape(shape[:-4] + (shape[-4] * 2,) + shape[-2:])
        bit //= 2
    shape = blocks.shape
    return blocks.reshape(shape[:-3] + (shape[-3] * shape[-2], shape[-1]))


def on_device(eigvecs, gauge_links, peramb, momenta, disp_paths, sources):
    num_vec = eigvecs.shape[-1]
    z_depth = eigvecs.shape[3]
    sites = eigvecs.shape[4]
    groups = lax.axis_size("gz")
    me = lax.axis_index("gz")
    lz_total = z_depth * groups
    row_count = num_vec // groups

    top = shifted(eigvecs[0, :, :, 0], "gz", -1)
    links = gauge_links[0].reshape(3, 18, z_depth, sites).transpose(0, 2, 1, 3)
    zcoord = me * z_depth + jnp.arange(z_depth, dtype=jnp.int32)
    angles = phase_angles(momenta, zcoord, lz_total).reshape(2, z_depth, sites)
    phases = jnp.stack([jnp.cos(angles), jnp.sin(angles)], axis=1)
    phases = phases.reshape(4, z_depth, sites).transpose(1, 0, 2)
    step = momenta.astype(F32) * (2.0 * math.pi / jnp.array([LX, LY, lz_total], F32))
    turn = jnp.stack([jnp.cos(step), jnp.sin(step)], axis=-1).reshape(2, 6)
    partial_value = partial_elementals(eigvecs, top, links, phases, turn, disp_paths)

    norm_scale = 1.0 / math.sqrt(12.0 * LX * LY * lz_total)
    slices = lax.axis_size("ta")
    if slices <= 16 and slices % 2 == 0 and groups == 4:
        rows_phi, held = exchange(partial_value.reshape(8, num_vec, num_vec), slices, norm_scale)
        rows_phi = rows_phi.reshape(2, 2, 2, row_count, num_vec)
    else:
        full_rows = lax.psum_scatter(partial_value, "gz", scatter_dimension=3, tiled=True)
        rows_phi = (full_rows * norm_scale).astype(BF16)
        held = gather_rows(lax.all_gather(rows_phi, "ta"))
    held = held.reshape(slices, 4, 2, num_vec, num_vec)
    picked = jnp.concatenate([lax.axis_index("ta")[None].astype(jnp.int32), sources])
    terms = correlator_terms(held, picked, peramb[0, :, 0])
    summed = lax.psum(jnp.sum(terms, axis=(-2, -1)), "gz") / (8.0 * num_vec)
    return (rows_phi[None], summed.reshape(-1, 1, 2, 2, 2))


def solution(mesh):
    placed = (
        P("ta", None, None, "gz", None, None),
        P("ta", None, None, None, None, "gz", None),
        P("ta", None, "gz", None, None, None, None),
        P(),
        P(),
        P(),
    )
    return jax.shard_map(
        on_device,
        mesh=mesh,
        in_specs=placed,
        out_specs=(P("ta", None, None, None, "gz", None), P(None, "ta", None, None, None)),
        check_vma=False,
    )
```
